32 devices in a mesh: grp: 1, ex: 32 (over z, y, x, core), ft: 1.
Axes of the slice: x: 2, y: 2, z: 4, core: 2. Of those that a mesh axis runs over, the one named last changes fastest.
Arguments:
- train_sketch: bfloat16 [4, 64, 16384], P(None, 'grp', 'ex'), may hold values from -6 to 6
- eval_sketch: bfloat16 [4, 128, 16384], P(None, 'grp', 'ex'), may hold values from -6 to 6
- projection: bfloat16 [16384, 4096], P('ex', 'ft'), may hold values from -0.046875 to 0.046875
- lr_weight: int32 [4], replicated, may hold values from 1 to 16
- train_ids: int32 [64], P(('grp', 'ex')), may hold values from 0 to 191
- eval_ids: int32 [128], P(('grp', 'ex')), may hold values from 0 to 191
Outputs:
- influence: float32 [64, 128], P(('grp', 'ex'), 'ft')
The draws below stay inside these ranges and needn't reach their ends.
All inputs are finite; a program needn't handle non-finite values.
Results may differ from the reference program's by a relative error of at most 0.0037.
Values may be sent and summed in bfloat16 or wider, within the bound.
A program may use at most 128 MiB of HBM per device.

```python
import jax
import jax.numpy as jnp
from jax import lax

SKETCH = 16384
FEATURES = 4096
CHECKPOINTS = 4
TRAIN_ROWS = 64
EVAL_ROWS = 128


def place_ends(result, own_key, low, top_value):
    index_at = [jax.random.randint(jax.random.fold_in(own_key, axis), (), 0, length) for axis, length in enumerate(result.shape)]
    main_axis = result.shape.index(max(result.shape))
    beside = index_at[:main_axis] + [(index_at[main_axis] + 1) % result.shape[main_axis]] + index_at[main_axis + 1:]
    return result.at[tuple(index_at)].set(low).at[tuple(beside)].set(top_value)


def strengthened(drawn, key, source, target, shards_of, factor):
    def block_of(axis_at):
        return (jnp.arange(drawn.shape[axis_at]) // (drawn.shape[axis_at] // shards_of)).reshape((-1,) + (1,) * (drawn.ndim - 1 - axis_at))

    first = jax.random.permutation(key, shards_of)[block_of(target)]
    second = (block_of(target) + shards_of // 2) % shards_of
    return jnp.where((block_of(source) == first) | (block_of(source) == second), factor * drawn, drawn)


def steps_of(stream_key, dims, cuts, least, high):
    loudness, own = 1.0, jax.random.fold_in(stream_key, 6)
    for axis_at, parts in cuts:
        heights = jnp.exp(jax.random.uniform(jax.random.fold_in(own, axis_at), (parts,), jnp.float32, least / len(cuts), high / len(cuts)))
        loudness = loudness * jnp.repeat(heights, dims[axis_at] // parts).reshape([-1 if axis == axis_at else 1 for axis in range(len(dims))])
    return loudness


def centred(rng, dims, spread, bound, shards=(), kind=jnp.bfloat16):
    level = steps_of(rng, dims, shards, -0.22, 0.18) if shards else 1.0
    values = jax.random.normal(rng, dims, jnp.float32) * spread * level
    return jnp.minimum(jnp.maximum(values, -bound), bound).astype(kind)


def bell_draw_with(rng, extent, deviation, most, pieces, heavy, kind=jnp.bfloat16):
    values = deviation * jax.random.normal(rng, extent, jnp.float32)
    if pieces:
        values = values * steps_of(rng, extent, pieces, -0.22, 0.18)
    return jnp.clip(strengthened(values, jax.random.fold_in(rng, 3), *heavy), -most, most).astype(kind)


def setup_inputs(seed: int = 0, part: int = 0) -> dict:
    arg_keys = jax.random.split(jax.random.key(seed), 7)
    own_keys = jax.random.split(jax.random.fold_in(arg_keys[6], part), 7)
    train_sketch = bell_draw_with(own_keys[0], (CHECKPOINTS, TRAIN_ROWS, SKETCH), 1.0, 6.0, ((2, 32),), (2, 1, 32, 2.75))
    eval_sketch = bell_draw_with(own_keys[1], (CHECKPOINTS, EVAL_ROWS, SKETCH), 1.0, 6.0, ((2, 32),), (2, 1, 32, 2.75))
    projection = centred(arg_keys[2], (SKETCH, FEATURES), SKETCH ** -0.5, 0.046875, ((0, 32),))
    lr_weight = place_ends(jax.random.randint(arg_keys[3], (CHECKPOINTS,), 1, 17), jax.random.fold_in(arg_keys[3], 1), 1, 16).astype(jnp.int32)
    train_ids = place_ends(jax.random.randint(own_keys[4], (TRAIN_ROWS,), 0, TRAIN_ROWS + EVAL_ROWS), jax.random.fold_in(own_keys[4], 1), 0, (TRAIN_ROWS + EVAL_ROWS) - 1).astype(jnp.int32)
    eval_ids = place_ends(jax.random.randint(own_keys[5], (EVAL_ROWS,), 0, TRAIN_ROWS + EVAL_ROWS), jax.random.fold_in(own_keys[5], 1), 0, (TRAIN_ROWS + EVAL_ROWS) - 1).astype(jnp.int32)
    return dict(train_sketch=train_sketch, eval_sketch=eval_sketch, projection=projection, lr_weight=lr_weight, train_ids=train_ids, eval_ids=eval_ids)


def normalize(projected):
    inverse = lax.rsqrt(lax.optimization_barrier(jnp.mean(projected * projected, axis=1, keepdims=True)) + 1e-06)
    return (projected * inverse).astype(jnp.bfloat16)

def reference(train_sketch, eval_sketch, projection, lr_weight, train_ids, eval_ids):
    total = jnp.zeros((TRAIN_ROWS, EVAL_ROWS), jnp.float32)
    for index in range(CHECKPOINTS):
        train_hat = normalize(jnp.dot(train_sketch[index], projection, preferred_element_type=jnp.float32))
        eval_hat = normalize(jnp.dot(eval_sketch[index], projection, preferred_element_type=jnp.float32))
        factor = lr_weight[index].astype(jnp.float32) / FEATURES
        total = total + factor * jnp.dot(train_hat, eval_hat.T, preferred_element_type=jnp.float32)
    same_example = train_ids[:, None] == eval_ids[None, :]
    return jnp.where(same_example, jnp.float32(0.0), total)
```

```python
import functools

import jax
import jax.numpy as jnp
from jax import lax
from jax.experimental import pallas as pl
from jax.experimental.pallas import tpu as pltpu
from jax.sharding import PartitionSpec as P

FEATURES = 4096


def project(sketch, projection):
    return lax.psum_scatter(
        jnp.dot(sketch, projection, preferred_element_type=jnp.float32),
        "ex",
        scatter_dimension=0,
        tiled=True,
    )


def add_block(totals, scores_block):
    return totals + scores_block


def shards(train_sketch, eval_sketch, projection, lr_weight, train_ids, eval_ids):
    checkpoints = train_sketch.shape[0]
    weights = lr_weight.astype(jnp.float32) / FEATURES
    train_proj = [project(train_sketch[index], projection) for index in range(checkpoints)]
    eval_proj = [project(eval_sketch[index], projection) for index in range(checkpoints)]
    train_squares = jnp.stack([jnp.sum(item * item, axis=1) for item in train_proj])
    eval_squares = jnp.stack([jnp.sum(item * item, axis=1) for item in eval_proj])
    train_total, eval_total = lax.psum((train_squares, eval_squares), "ft")
    train_inv = lax.rsqrt(train_total / FEATURES + 1e-06)
    eval_inv = lax.rsqrt(eval_total / FEATURES + 1e-06)
    train_hats = [
        (train_proj[index] * train_inv[index][:, None]).astype(jnp.bfloat16)
        for index in range(checkpoints)
    ]
    eval_hats = [
        (eval_proj[index] * eval_inv[index][:, None]).astype(jnp.bfloat16)
        for index in range(checkpoints)
    ]
    eval_total_rows = eval_ids.shape[0] * lax.axis_size("ex")
    initial = jnp.zeros((train_ids.shape[0], eval_total_rows), jnp.float32)
    scores = initial
    for index in range(checkpoints):
        features_block = lax.all_gather(eval_hats[index], "ex", axis=0, tiled=True)
        fold_eval_block = lax.all_gather(eval_ids, "ex", axis=0, tiled=True)
        fold_scores_block = weights[index] * jnp.einsum(
            "ik,jk->ij", train_hats[index], features_block, preferred_element_type=jnp.float32
        )
        same_example = train_ids[:, None] == fold_eval_block[None, :]
        scores = add_block(scores, jnp.where(same_example, jnp.float32(0.0), fold_scores_block))
    return lax.psum_scatter(scores, "ft", scatter_dimension=1, tiled=True)


LINK = jnp.bfloat16
MESH_ID = pl.DeviceIdType.MESH
HIGHEST = lax.Precision.HIGHEST
OFFSETS = (2, 1, 3, 0)
STEPS = len(OFFSETS)
BLOCK = 128


def coded(value):
    return (value * jnp.abs(value)).astype(LINK)


def decoded(code):
    wide = code.astype(jnp.float32)
    return wide * lax.rsqrt(jnp.maximum(jnp.abs(wide), jnp.float32(1e-36)))


def other(value):
    return 1 - value


def device_at(z, y, x, core):
    return ((z * 2 + y) * 2 + x) * 2 + core


def send(src, dst, send_sem, recv_sem, device):
    copy = pltpu.make_async_remote_copy(
        src_ref=src,
        dst_ref=dst,
        send_sem=send_sem,
        recv_sem=recv_sem,
        device_id={"ex": device},
        device_id_type=MESH_ID,
    )
    copy.start()
    return copy


def influence_kernel(
    train_ref,
    eval_ref,
    proj_ref,
    lr_ref,
    train_ids_ref,
    eval_ids_ref,
    out_ref,
    sk_own,
    sk_sib,
    pr_own,
    pr_sib,
    s1a,
    s1b,
    r1a,
    r1b,
    keep_a,
    keep_b,
    s2a,
    s2b,
    r2a,
    r2b,
    sz,
    rz,
    fin,
    tperm,
    p1,
    r1p,
    acc,
    p2,
    r2p,
    local_sem,
    pr_sem,
    sib_send,
    sib_recv,
    psib_send,
    psib_recv,
    s1_send,
    s1_recv,
    s2_send,
    s2_recv,
    z_send,
    z_recv,
    p1_send,
    p1_recv,
    p2_send,
    p2_recv,
):
    me = lax.axis_index("ex")
    core = lax.rem(me, 2)
    x = lax.rem(me // 2, 2)
    y = lax.rem(me // 4, 2)
    z = me // 8
    sib = device_at(z, y, x, other(core))
    x_dev = device_at(z, y, other(x), core)
    y_dev = device_at(z, other(y), x, core)
    plane = [
        ((y + dy) % 2, (x + dx) % 2, (core + dc) % 2)
        for dy in range(2)
        for dx in range(2)
        for dc in range(2)
    ][1:]
    checkpoints = lr_ref.shape[0]
    train_rows = train_ref.shape[0]
    rows = sk_own.shape[0]
    half_rows = rows // 2
    step_cols = 4 * BLOCK
    half_cols = STEPS * step_cols
    features = 2 * half_cols
    zs = [lax.rem(z + offset, 4) for offset in OFFSETS]

    own_sketch = [
        pltpu.make_async_copy(train_ref, sk_own.at[pl.ds(0, train_rows)], local_sem.at[0]),
        pltpu.make_async_copy(
            eval_ref, sk_own.at[pl.ds(train_rows, rows - train_rows)], local_sem.at[1]
        ),
    ]
    for copy in own_sketch:
        copy.start()
    own_proj = []
    for k in range(STEPS):
        start = pl.multiple_of(core * half_cols + zs[k] * step_cols, step_cols)
        copy = pltpu.make_async_copy(
            proj_ref.at[:, pl.ds(start, step_cols)], pr_own.at[k], pr_sem.at[k]
        )
        copy.start()
        own_proj.append(copy)

    barrier = pltpu.get_barrier_semaphore()
    partners = [device_at(z, *place) for place in plane]
    partners += [device_at(lax.rem(z + offset, 4), y, x, core) for offset in (1, 2, 3)]
    for partner in partners:
        pl.semaphore_signal(barrier, inc=1, device_id={"ex": partner}, device_id_type=MESH_ID)
    pl.semaphore_wait(barrier, len(partners))

    sib_copies = [
        send(train_ref, sk_sib.at[pl.ds(0, train_rows)], sib_send.at[0], sib_recv.at[0], sib),
        send(
            eval_ref,
            sk_sib.at[pl.ds(train_rows, rows - train_rows)],
            sib_send.at[1],
            sib_recv.at[1],
            sib,
        ),
    ]
    psib_copies = []
    for k in range(STEPS):
        start = pl.multiple_of(other(core) * half_cols + zs[k] * step_cols, step_cols)
        psib_copies.append(
            send(
                proj_ref.at[:, pl.ds(start, step_cols)],
                pr_sib.at[k],
                psib_send.at[k],
                psib_recv.at[k],
                sib,
            )
        )
    for copy in own_sketch:
        copy.wait()
    for copy in sib_copies:
        copy.wait_recv()

    s1_copies, s2_copies, z_copies = {}, {}, {}

    def projected(k, side, first):
        part = pl.ds(first, half_rows)
        cols = pl.ds(pl.multiple_of(side * 2 * BLOCK, 2 * BLOCK), 2 * BLOCK)
        total = jnp.dot(
            sk_own[part, :], pr_own[k, :, cols], preferred_element_type=jnp.float32
        ) + jnp.dot(sk_sib[part, :], pr_sib[k, :, cols], preferred_element_type=jnp.float32)
        low, high = total[:, :BLOCK], total[:, BLOCK:]
        return jnp.where(y == 0, high, low), jnp.where(y == 0, low, high)

    def first(k):
        own_proj[k].wait()
        psib_copies[k].wait_recv()
        far, near = projected(k, other(x), 0)
        s1a[k, 0] = coded(far)
        s1a[k, 1] = coded(near)
        copy_a = send(s1a.at[k], r1a.at[k], s1_send.at[0, k], s1_recv.at[0, k], x_dev)
        far, near = projected(k, other(x), half_rows)
        s1b[k, 0] = coded(far)
        keep_b[k, 0] = near
        far, near = projected(k, x, half_rows)
        s1b[k, 1] = coded(far)
        keep_b[k, 1] = near
        copy_b = send(s1b.at[k], r1b.at[k], s1_send.at[1, k], s1_recv.at[1, k], y_dev)
        far, near = projected(k, x, 0)
        keep_a[k, 0] = far
        keep_a[k, 1] = near
        s1_copies[k] = (copy_a, copy_b)

    def second(k):
        s1_copies[k][0].wait_recv()
        s2a[k] = coded(keep_a[k, 0] + decoded(r1a[k, 0]))
        copy_a = send(s2a.at[k], r2a.at[k], s2_send.at[0, k], s2_recv.at[0, k], y_dev)
        s1_copies[k][1].wait_recv()
        s2b[k] = coded(keep_b[k, 0] + decoded(r1b[k, 0]))
        copy_b = send(s2b.at[k], r2b.at[k], s2_send.at[1, k], s2_recv.at[1, k], x_dev)
        keep_a[k, 1] += decoded(r1a[k, 1])
        keep_b[k, 1] += decoded(r1b[k, 1])
        s2_copies[k] = (copy_a, copy_b)

    def third(k):
        for copy in s2_copies[k]:
            copy.wait_recv()
        part_a = keep_a[k, 1] + decoded(r2a[k])
        part_b = keep_b[k, 1] + decoded(r2b[k])
        if OFFSETS[k] == 0:
            fin[pl.ds(0, half_rows), :] = part_a
            fin[pl.ds(half_rows, half_rows), :] = part_b
        else:
            sz[k, pl.ds(0, half_rows), :] = coded(part_a)
            sz[k, pl.ds(half_rows, half_rows), :] = coded(part_b)
            z_copies[k] = send(
                sz.at[k], rz.at[k], z_send.at[k], z_recv.at[k], device_at(zs[k], y, x, core)
            )

    first(0)
    first(1)
    second(0)
    first(2)
    second(1)
    third(0)
    first(3)
    second(2)
    third(1)
    second(3)
    third(2)
    third(3)
    for k in z_copies:
        z_copies[k].wait_recv()
    fin[...] += (
        decoded(rz[0]) + decoded(rz[1]) + decoded(rz[2])
    )

    per_checkpoint = train_rows // checkpoints
    eval_rows = (rows - train_rows) // checkpoints
    for c in range(checkpoints):
        for z_at in range(4):
            for p in range(8):
                tperm[c, p * 8 + z_at * 2 : p * 8 + z_at * 2 + 2, :] = fin[
                    c * per_checkpoint + z_at * 16 + p * 2 : c * per_checkpoint + z_at * 16 + p * 2 + 2, :
                ]
    lane = lax.broadcasted_iota(jnp.int32, (per_checkpoint, BLOCK), 1)
    row8 = lax.broadcasted_iota(jnp.int32, (8, BLOCK), 0)
    lane8 = lax.broadcasted_iota(jnp.int32, (8, BLOCK), 1)
    ones = jnp.ones((8, BLOCK), jnp.float32)
    train_squares = jnp.zeros((per_checkpoint, BLOCK), jnp.float32)
    shared = jnp.zeros((8, BLOCK), jnp.float32)
    contract = (((1,), (1,)), ((), ()))
    for c in range(checkpoints):
        train_c = tperm[c]
        eval_c = fin[train_rows + c * eval_rows : train_rows + (c + 1) * eval_rows, :]
        scores = lax.dot_general(
            train_c, eval_c, contract, precision=HIGHEST, preferred_element_type=jnp.float32
        )
        for p in range(8):
            p1[p, c] = scores[p * 8 : (p + 1) * 8, :]
        squares = jnp.sum(train_c * train_c, axis=1, keepdims=True)
        train_squares = jnp.where(lane == c, squares, train_squares)
        eval_squares = lax.dot_general(
            ones, eval_c * eval_c, contract, precision=HIGHEST, preferred_element_type=jnp.float32
        )
        shared = jnp.where(row8 == 2 + c, eval_squares, shared)
    own_ids = eval_ids_ref.shape[0]
    for at in range(own_ids):
        place = (row8 == 6) & (lane8 == me * own_ids + at)
        shared = jnp.where(place, eval_ids_ref[at].astype(jnp.float32), shared)
    for p in range(8):
        p1[p, 4] = train_squares[p * 8 : (p + 1) * 8, :]
        p1[p, 5] = shared

    p1_copies = []
    for at, (y_at, x_at, core_at) in enumerate(plane):
        p1_copies.append(
            send(
                p1.at[(y_at * 2 + x_at) * 2 + core_at],
                r1p.at[at],
                p1_send.at[at],
                p1_recv.at[at],
                device_at(z, y_at, x_at, core_at),
            )
        )
    total = p1[lax.rem(me, 8)]
    for at, copy in enumerate(p1_copies):
        copy.wait_recv()
        total = total + r1p[at]
    acc[...] = total
    for z_at in range(4):
        for c in range(checkpoints):
            p2[z_at, 0, 2 * c : 2 * c + 2, :] = acc[c, 2 * z_at : 2 * z_at + 2, :]
        p2[z_at, 1] = acc[5]
        p2[z_at, 1, 0:2, :] = acc[4, 2 * z_at : 2 * z_at + 2, :]
    p2_copies = []
    for at in range(3):
        to = lax.rem(z + at + 1, 4)
        p2_copies.append(
            send(
                p2.at[to], r2p.at[at], p2_send.at[at], p2_recv.at[at], device_at(to, y, x, core)
            )
        )
    total = p2[z]
    for at, copy in enumerate(p2_copies):
        copy.wait_recv()
        total = total + r2p[at]
    raw, rest = total[0], total[1]
    result = jnp.zeros((2, BLOCK), jnp.float32)
    for c in range(checkpoints):
        weight = lr_ref[c].astype(jnp.float32) / features
        train_inv = lax.rsqrt(rest[0:2, c : c + 1] / features + 1e-06)
        eval_inv = lax.rsqrt(rest[2 + c : 3 + c, :] / features + 1e-06)
        result = result + weight * (raw[2 * c : 2 * c + 2, :] * train_inv * eval_inv)
    ids = rest[6:7, :]
    row2 = lax.broadcasted_iota(jnp.int32, (2, BLOCK), 0)
    own = jnp.where(
        row2 == 0, train_ids_ref[0].astype(jnp.float32), train_ids_ref[1].astype(jnp.float32)
    )
    out_ref[...] = jnp.where(own == ids, jnp.float32(0.0), result)

    for copy in sib_copies + psib_copies + p1_copies + p2_copies:
        copy.wait_send()
    for group in (s1_copies, s2_copies):
        for k in group:
            for copy in group[k]:
                copy.wait_send()
    for k in z_copies:
        z_copies[k].wait_send()


def fused(train_sketch, eval_sketch, projection, lr_weight, train_ids, eval_ids):
    checkpoints, train_rows, depth = train_sketch.shape
    eval_rows = eval_sketch.shape[1]
    rows = checkpoints * (train_rows + eval_rows)
    half = rows // 2
    step_cols = 4 * BLOCK
    anywhere = pl.BlockSpec(memory_space=pl.ANY)
    scalars = pl.BlockSpec(memory_space=pltpu.SMEM)
    dma = pltpu.SemaphoreType.DMA
    f32, bf16 = jnp.float32, jnp.bfloat16
    return pl.pallas_call(
        influence_kernel,
        out_shape=jax.ShapeDtypeStruct((train_ids.shape[0], eval_rows), f32),
        in_specs=[anywhere] * 3 + [scalars] * 3,
        out_specs=pl.BlockSpec(memory_space=pltpu.VMEM),
        scratch_shapes=[
            pltpu.VMEM((rows, depth), bf16),
            pltpu.VMEM((rows, depth), bf16),
            pltpu.VMEM((STEPS, depth, step_cols), bf16),
            pltpu.VMEM((STEPS, depth, step_cols), bf16),
            pltpu.VMEM((STEPS, 2, half, BLOCK), LINK),
            pltpu.VMEM((STEPS, 2, half, BLOCK), LINK),
            pltpu.VMEM((STEPS, 2, half, BLOCK), LINK),
            pltpu.VMEM((STEPS, 2, half, BLOCK), LINK),
            pltpu.VMEM((STEPS, 2, half, BLOCK), f32),
            pltpu.VMEM((STEPS, 2, half, BLOCK), f32),
            pltpu.VMEM((STEPS, half, BLOCK), LINK),
            pltpu.VMEM((STEPS, half, BLOCK), LINK),
            pltpu.VMEM((STEPS, half, BLOCK), LINK),
            pltpu.VMEM((STEPS, half, BLOCK), LINK),
            pltpu.VMEM((3, rows, BLOCK), LINK),
            pltpu.VMEM((3, rows, BLOCK), LINK),
            pltpu.VMEM((rows, BLOCK), f32),
            pltpu.VMEM((checkpoints, train_rows, BLOCK), f32),
            pltpu.VMEM((8, 6, 8, BLOCK), f32),
            pltpu.VMEM((7, 6, 8, BLOCK), f32),
            pltpu.VMEM((6, 8, BLOCK), f32),
            pltpu.VMEM((4, 2, 8, BLOCK), f32),
            pltpu.VMEM((3, 2, 8, BLOCK), f32),
            dma((2,)),
            dma((STEPS,)),
            dma((2,)),
            dma((2,)),
            dma((STEPS,)),
            dma((STEPS,)),
            dma((2, STEPS)),
            dma((2, STEPS)),
            dma((2, STEPS)),
            dma((2, STEPS)),
            dma((3,)),
            dma((3,)),
            dma((7,)),
            dma((7,)),
            dma((3,)),
            dma((3,)),
        ],
        compiler_params=pltpu.CompilerParams(
            collective_id=0, has_side_effects=True, vmem_limit_bytes=48 * 1024 * 1024
        ),
    )(
        train_sketch.reshape(checkpoints * train_rows, depth),
        eval_sketch.reshape(checkpoints * eval_rows, depth),
        projection,
        lr_weight,
        train_ids,
        eval_ids,
    )


def planned(mesh):
    def body(train_sketch, eval_sketch, projection, lr_weight, train_ids, eval_ids):
        arrays = (train_sketch, eval_sketch, projection, lr_weight, train_ids, eval_ids)
        sizes = (mesh.shape["grp"], mesh.shape["ex"], mesh.shape["ft"])
        fits = (
            sizes == (1, 32, 1)
            and train_sketch.shape[:2] == (4, 64)
            and eval_sketch.shape[:2] == (4, 128)
            and projection.shape[1] == FEATURES == 2 * STEPS * 4 * BLOCK
        )
        return fused(*arrays) if fits else shards(*arrays)

    return body


def solution(mesh):
    body = planned(mesh)
    return jax.shard_map(
        body,
        mesh=mesh,
        in_specs=(
            P(None, "grp", "ex"),
            P(None, "grp", "ex"),
            P("ex", "ft"),
            P(),
            P(("grp", "ex")),
            P(("grp", "ex")),
        ),
        out_specs=P(("grp", "ex"), "ft"),
        check_vma=False,
    )
```

```python
import functools

import jax
import jax.numpy as jnp
from jax import lax
from jax.experimental import pallas as pl
from jax.experimental.pallas import tpu as pltpu
from jax.sharding import PartitionSpec as P

FEATURES = 4096


def project(sketch, projection):
    return lax.psum_scatter(
        jnp.dot(sketch, projection, preferred_element_type=jnp.float32),
        "ex",
        scatter_dimension=0,
        tiled=True,
    )


def add_block(totals, scores_block):
    return totals + scores_block


def shards(train_sketch, eval_sketch, projection, lr_weight, train_ids, eval_ids):
    checkpoints = train_sketch.shape[0]
    weights = lr_weight.astype(jnp.float32) / FEATURES
    train_proj = [project(train_sketch[index], projection) for index in range(checkpoints)]
    eval_proj = [project(eval_sketch[index], projection) for index in range(checkpoints)]
    train_squares = jnp.stack([jnp.sum(item * item, axis=1) for item in train_proj])
    eval_squares = jnp.stack([jnp.sum(item * item, axis=1) for item in eval_proj])
    train_total, eval_total = lax.psum((train_squares, eval_squares), "ft")
    train_inv = lax.rsqrt(train_total / FEATURES + 1e-06)
    eval_inv = lax.rsqrt(eval_total / FEATURES + 1e-06)
    train_hats = [
        (train_proj[index] * train_inv[index][:, None]).astype(jnp.bfloat16)
        for index in range(checkpoints)
    ]
    eval_hats = [
        (eval_proj[index] * eval_inv[index][:, None]).astype(jnp.bfloat16)
        for index in range(checkpoints)
    ]
    eval_total_rows = eval_ids.shape[0] * lax.axis_size("ex")
    initial = jnp.zeros((train_ids.shape[0], eval_total_rows), jnp.float32)
    scores = initial
    for index in range(checkpoints):
        features_block = lax.all_gather(eval_hats[index], "ex", axis=0, tiled=True)
        fold_eval_block = lax.all_gather(eval_ids, "ex", axis=0, tiled=True)
        fold_scores_block = weights[index] * jnp.einsum(
            "ik,jk->ij", train_hats[index], features_block, preferred_element_type=jnp.float32
        )
        same_example = train_ids[:, None] == fold_eval_block[None, :]
        scores = add_block(scores, jnp.where(same_example, jnp.float32(0.0), fold_scores_block))
    return lax.psum_scatter(scores, "ft", scatter_dimension=1, tiled=True)


LINK = jnp.bfloat16
MESH_ID = pl.DeviceIdType.MESH
HIGHEST = lax.Precision.HIGHEST
OFFSETS = (2, 1, 3, 0)
STEPS = len(OFFSETS)
LANES = 128
TILE = 256


def coded(value):
    return (value * jnp.abs(value)).astype(LINK)


def decoded(code):
    wide = code.astype(jnp.float32)
    return wide * lax.rsqrt(jnp.maximum(jnp.abs(wide), jnp.float32(1e-36)))


def other(value):
    return 1 - value


def device_at(z, y, x, core):
    return ((z * 2 + y) * 2 + x) * 2 + core


def send(src, dst, send_sem, recv_sem, device):
    copy = pltpu.make_async_remote_copy(
        src_ref=src,
        dst_ref=dst,
        send_sem=send_sem,
        recv_sem=recv_sem,
        device_id={"ex": device},
        device_id_type=MESH_ID,
    )
    copy.start()
    return copy


def influence_kernel(
    train_ref,
    eval_ref,
    proj_ref,
    lr_ref,
    train_ids_ref,
    eval_ids_ref,
    out_ref,
    sketch,
    proj,
    s0,
    r0,
    keep,
    s1a,
    s1b,
    r1a,
    r1b,
    s2a,
    s2b,
    r2a,
    r2b,
    sz,
    rz,
    fin,
    scores_ref,
    p1,
    r1p,
    scaled_ref,
    p2,
    r2p,
    local_sem,
    pr_sem,
    s0_send,
    s0_recv,
    s1_send,
    s1_recv,
    s2_send,
    s2_recv,
    z_send,
    z_recv,
    p1_send,
    p1_recv,
    p2_send,
    p2_recv,
    ready,
):
    me = lax.axis_index("ex")
    core = lax.rem(me, 2)
    x = lax.rem(me // 2, 2)
    y = lax.rem(me // 4, 2)
    z = me // 8
    sib = device_at(z, y, x, other(core))
    x_dev = device_at(z, y, other(x), core)
    y_dev = device_at(z, other(y), x, core)
    plane = [
        ((y + dy) % 2, (x + dx) % 2, (core + dc) % 2)
        for dy in range(2)
        for dx in range(2)
        for dc in range(2)
    ][:0:-1]
    checkpoints = lr_ref.shape[0]
    train_rows = train_ref.shape[0] // checkpoints
    eval_rows = eval_ref.shape[0] // checkpoints
    rows = train_rows + eval_rows
    all_train = checkpoints * train_rows
    block = keep.shape[3]
    half_cols = 4 * block
    part_a, part_b = pl.ds(0, rows // 2), pl.ds(rows // 2, rows // 2)
    zs = [lax.rem(z + offset, 4) for offset in OFFSETS]

    own_sketch = [
        pltpu.make_async_copy(train_ref, sketch.at[pl.ds(0, all_train)], local_sem.at[0]),
        pltpu.make_async_copy(
            eval_ref, sketch.at[pl.ds(all_train, checkpoints * eval_rows)], local_sem.at[1]
        ),
    ]
    for copy in own_sketch:
        copy.start()
    own_proj = []
    for at, side in enumerate((other(core), core)):
        for part in range(2):
            start = pl.multiple_of(side * half_cols + part * 2 * block, 2 * block)
            copy = pltpu.make_async_copy(
                proj_ref.at[:, pl.ds(start, 2 * block)], proj.at[at, part], pr_sem.at[at, part]
            )
            copy.start()
            own_proj.append(copy)

    below, above = z > 0, z < 3
    z_neighbours = below.astype(jnp.int32) + above.astype(jnp.int32)

    def signal(semaphore, device):
        pl.semaphore_signal(semaphore, inc=1, device_id={"ex": device}, device_id_type=MESH_ID)

    def signal_z(semaphore):
        @pl.when(below)
        def _():
            signal(semaphore, device_at(z - 1, y, x, core))

        @pl.when(above)
        def _():
            signal(semaphore, device_at(z + 1, y, x, core))

    barrier = pltpu.get_barrier_semaphore()
    for partner in (sib, x_dev, y_dev):
        signal(barrier, partner)
    signal_z(barrier)

    for copy in own_sketch:
        copy.wait()

    def product(at, tile, store):
        per_part = 2 * block // TILE
        part, first_col = tile // per_part, tile % per_part * TILE
        if first_col == 0:
            own_proj[2 * at + part].wait()
        total = jnp.dot(
            sketch[...],
            proj[at, part, :, first_col : first_col + TILE],
            preferred_element_type=jnp.float32,
        )
        per_block = block // TILE
        to, cols = tile // per_block, pl.ds(tile % per_block * TILE, TILE)
        for c in range(checkpoints):
            store(c, to, pl.ds(0, train_rows), cols, total[c * train_rows : (c + 1) * train_rows])
            low = all_train + c * eval_rows
            store(c, to, pl.ds(train_rows, eval_rows), cols, total[low : low + eval_rows])

    def store_sent(c, to, place, cols, value):
        s0[c, to, place, cols] = coded(value)

    def store_kept(c, to, place, cols, value):
        keep[c, to, place, cols] = value

    tiles = half_cols // TILE
    for tile in range(tiles):
        product(0, tile, store_sent)
    pl.semaphore_wait(barrier, 3 + z_neighbours)
    signal_z(ready.at[0])

    s0_copies, s1_copies, s2_copies, z_copies = {}, {}, {}, {}

    def swap(k):
        c = zs[k]
        s0_copies[k] = send(s0.at[c], r0.at[c], s0_send.at[k], s0_recv.at[k], sib)

    def summed(c, at, part):
        return keep[c, at, part, :] + decoded(r0[c, at, part, :])

    def first(k):
        c = zs[k]
        s0_copies[k].wait_recv()
        for slot, y_at in enumerate((other(y), y)):
            s1a[k, slot] = coded(summed(c, other(x) * 2 + y_at, part_a))
        copy_a = send(s1a.at[k], r1a.at[k], s1_send.at[0, k], s1_recv.at[0, k], x_dev)
        for slot, x_at in enumerate((other(x), x)):
            s1b[k, slot] = coded(summed(c, x_at * 2 + other(y), part_b))
        copy_b = send(s1b.at[k], r1b.at[k], s1_send.at[1, k], s1_recv.at[1, k], y_dev)
        for y_at in (other(y), y):
            keep[c, x * 2 + y_at, part_a, :] = summed(c, x * 2 + y_at, part_a)
        for x_at in (other(x), x):
            keep[c, x_at * 2 + y, part_b, :] = summed(c, x_at * 2 + y, part_b)
        s1_copies[k] = (copy_a, copy_b)

    def second(k):
        c = zs[k]
        s1_copies[k][0].wait_recv()
        s2a[k] = coded(keep[c, x * 2 + other(y), part_a, :] + decoded(r1a[k, 0]))
        copy_a = send(s2a.at[k], r2a.at[k], s2_send.at[0, k], s2_recv.at[0, k], y_dev)
        s1_copies[k][1].wait_recv()
        s2b[k] = coded(keep[c, other(x) * 2 + y, part_b, :] + decoded(r1b[k, 0]))
        copy_b = send(s2b.at[k], r2b.at[k], s2_send.at[1, k], s2_recv.at[1, k], x_dev)
        keep[c, x * 2 + y, part_a, :] += decoded(r1a[k, 1])
        keep[c, x * 2 + y, part_b, :] += decoded(r1b[k, 1])
        s2_copies[k] = (copy_a, copy_b)

    def third(k):
        c = zs[k]
        for copy, received, part in zip(s2_copies[k], (r2a, r2b), (part_a, part_b)):
            copy.wait_recv()
            value = keep[c, x * 2 + y, part, :] + decoded(received[k])
            if OFFSETS[k] == 0:
                fin[part, :] = value
            else:
                sz[k, part, :] = coded(value)
        if OFFSETS[k]:
            z_copies[k] = send(
                sz.at[k], rz.at[k], z_send.at[k], z_recv.at[k], device_at(c, y, x, core)
            )

    swap(0)
    swap(1)
    for tile in range(tiles):
        product(1, tile, store_kept)
    first(0)
    swap(2)
    first(1)
    swap(3)
    second(0)
    first(2)
    pl.semaphore_wait(ready.at[0], z_neighbours)
    signal_z(ready.at[1])
    second(1)
    pl.semaphore_wait(ready.at[1], z_neighbours)
    third(0)
    first(3)
    second(2)
    third(1)
    second(3)
    third(2)
    third(3)
    for k in z_copies:
        z_copies[k].wait_recv()
        fin[...] += decoded(rz[k])

    train = fin[pl.ds(0, train_rows), :]
    evals = fin[pl.ds(train_rows, eval_rows), :]
    contract = (((1,), (1,)), ((), ()))

    def dot(left, right):
        return lax.dot_general(
            left, right, contract, precision=HIGHEST, preferred_element_type=jnp.float32
        )

    scores_ref[...] = dot(train, evals)
    ones = jnp.ones((8, block), jnp.float32)
    train_squares = dot(ones, train * train)
    eval_squares = dot(ones, evals * evals)
    row8 = lax.broadcasted_iota(jnp.int32, (8, LANES), 0)
    lane8 = lax.broadcasted_iota(jnp.int32, (8, LANES), 1)
    shared = jnp.where(row8 == 3, eval_squares, jnp.float32(0.0))
    own_ids = eval_ids_ref.shape[0]
    for at in range(own_ids):
        place = (row8 == 2) & (lane8 == me * own_ids + at)
        shared = jnp.where(place, eval_ids_ref[at].astype(jnp.float32), shared)
    for p in range(8):
        for z_at in range(4):
            low = z_at * 16 + p * 2
            p1[p, 0, z_at * 2 : z_at * 2 + 2, :] = scores_ref[low : low + 2, :]
        p1[p, 1] = shared
        p1[p, 1, 4:5, 0:train_rows] = train_squares[0:1, :]

    p1_copies = []
    for at, (y_at, x_at, core_at) in enumerate(plane):
        p1_copies.append(
            send(
                p1.at[(y_at * 2 + x_at) * 2 + core_at],
                r1p.at[at],
                p1_send.at[at],
                p1_recv.at[at],
                device_at(z, y_at, x_at, core_at),
            )
        )
    total = p1[lax.rem(me, 8)]
    for at, copy in reversed(list(enumerate(p1_copies))):
        copy.wait_recv()
        total = total + r1p[at]
    shared = total[1]
    owner_lane = row8 // 2 * 16 + lax.rem(me, 8) * 2 + row8 % 2
    train_square = jnp.sum(
        jnp.where(lane8 == owner_lane, shared[4:5, :], jnp.float32(0.0)), axis=1, keepdims=True
    )
    weight = lr_ref[z].astype(jnp.float32) / FEATURES
    train_inv = lax.rsqrt(train_square / FEATURES + 1e-06)
    eval_inv = lax.rsqrt(shared[3:4, :] / FEATURES + 1e-06)
    scaled_ref[...] = weight * (total[0] * train_inv * eval_inv)
    for z_at in range(4):
        p2[z_at] = shared
        p2[z_at, 0:2, :] = scaled_ref[2 * z_at : 2 * z_at + 2, :]
    p2_copies = []
    for at in range(3):
        to = lax.rem(z + at + 1, 4)
        p2_copies.append(
            send(
                p2.at[to], r2p.at[at], p2_send.at[at], p2_recv.at[at], device_at(to, y, x, core)
            )
        )
    total = p2[z]
    for at, copy in enumerate(p2_copies):
        copy.wait_recv()
        total = total + r2p[at]
    row2 = lax.broadcasted_iota(jnp.int32, (2, LANES), 0)
    own = jnp.where(
        row2 == 0, train_ids_ref[0].astype(jnp.float32), train_ids_ref[1].astype(jnp.float32)
    )
    out_ref[...] = jnp.where(own == total[2:3, :], jnp.float32(0.0), total[0:2, :])

    for copy in p1_copies + p2_copies:
        copy.wait_send()
    for k in range(STEPS):
        s0_copies[k].wait_send()
        for copy in s1_copies[k] + s2_copies[k]:
            copy.wait_send()
    for k in z_copies:
        z_copies[k].wait_send()


def fused(train_sketch, eval_sketch, projection, lr_weight, train_ids, eval_ids):
    checkpoints, train_rows, depth = train_sketch.shape
    eval_rows = eval_sketch.shape[1]
    rows = train_rows + eval_rows
    half = rows // 2
    block = projection.shape[1] // 8
    anywhere = pl.BlockSpec(memory_space=pl.ANY)
    scalars = pl.BlockSpec(memory_space=pltpu.SMEM)
    dma = pltpu.SemaphoreType.DMA
    f32, bf16 = jnp.float32, jnp.bfloat16
    return pl.pallas_call(
        influence_kernel,
        out_shape=jax.ShapeDtypeStruct((train_ids.shape[0], eval_rows), f32),
        in_specs=[anywhere] * 3 + [scalars] * 3,
        out_specs=pl.BlockSpec(memory_space=pltpu.VMEM),
        scratch_shapes=[
            pltpu.VMEM((checkpoints * rows, depth), bf16),
            pltpu.VMEM((2, 2, depth, 2 * block), bf16),
            pltpu.VMEM((checkpoints, 4, rows, block), LINK),
            pltpu.VMEM((checkpoints, 4, rows, block), LINK),
            pltpu.VMEM((checkpoints, 4, rows, block), f32),
            pltpu.VMEM((STEPS, 2, half, block), LINK),
            pltpu.VMEM((STEPS, 2, half, block), LINK),
            pltpu.VMEM((STEPS, 2, half, block), LINK),
            pltpu.VMEM((STEPS, 2, half, block), LINK),
            pltpu.VMEM((STEPS, half, block), LINK),
            pltpu.VMEM((STEPS, half, block), LINK),
            pltpu.VMEM((STEPS, half, block), LINK),
            pltpu.VMEM((STEPS, half, block), LINK),
            pltpu.VMEM((3, rows, block), LINK),
            pltpu.VMEM((3, rows, block), LINK),
            pltpu.VMEM((rows, block), f32),
            pltpu.VMEM((train_rows, LANES), f32),
            pltpu.VMEM((8, 2, 8, LANES), f32),
            pltpu.VMEM((7, 2, 8, LANES), f32),
            pltpu.VMEM((8, LANES), f32),
            pltpu.VMEM((4, 8, LANES), f32),
            pltpu.VMEM((3, 8, LANES), f32),
            dma((2,)),
            dma((2, 2)),
            dma((STEPS,)),
            dma((STEPS,)),
            dma((2, STEPS)),
            dma((2, STEPS)),
            dma((2, STEPS)),
            dma((2, STEPS)),
            dma((3,)),
            dma((3,)),
            dma((7,)),
            dma((7,)),
            dma((3,)),
            dma((3,)),
            pltpu.SemaphoreType.REGULAR((2,)),
        ],
        compiler_params=pltpu.CompilerParams(
            collective_id=0, has_side_effects=True, vmem_limit_bytes=60 * 1024 * 1024
        ),
    )(
        train_sketch.reshape(checkpoints * train_rows, depth),
        eval_sketch.reshape(checkpoints * eval_rows, depth),
        projection,
        lr_weight,
        train_ids,
        eval_ids,
    )


def planned(mesh):
    def body(train_sketch, eval_sketch, projection, lr_weight, train_ids, eval_ids):
        arrays = (train_sketch, eval_sketch, projection, lr_weight, train_ids, eval_ids)
        sizes = (mesh.shape["grp"], mesh.shape["ex"], mesh.shape["ft"])
        fits = (
            sizes == (1, 32, 1)
            and train_sketch.shape[:2] == (4, 64)
            and eval_sketch.shape[:2] == (4, 128)
            and projection.shape[1] == FEATURES
        )
        return fused(*arrays) if fits else shards(*arrays)

    return body


def solution(mesh):
    body = planned(mesh)
    return jax.shard_map(
        body,
        mesh=mesh,
        in_specs=(
            P(None, "grp", "ex"),
            P(None, "grp", "ex"),
            P("ex", "ft"),
            P(),
            P(("grp", "ex")),
            P(("grp", "ex")),
        ),
        out_specs=P(("grp", "ex"), "ft"),
        check_vma=False,
    )
```

```python
import functools

import jax
import jax.numpy as jnp
from jax import lax
from jax.experimental import pallas as pl
from jax.experimental.pallas import tpu as pltpu
from jax.sharding import PartitionSpec as P

FEATURES = 4096


def project(sketch, projection):
    return lax.psum_scatter(
        jnp.dot(sketch, projection, preferred_element_type=jnp.float32),
        "ex",
        scatter_dimension=0,
        tiled=True,
    )


def add_block(totals, scores_block):
    return totals + scores_block


def shards(train_sketch, eval_sketch, projection, lr_weight, train_ids, eval_ids):
    checkpoints = train_sketch.shape[0]
    weights = lr_weight.astype(jnp.float32) / FEATURES
    train_proj = [project(train_sketch[index], projection) for index in range(checkpoints)]
    eval_proj = [project(eval_sketch[index], projection) for index in range(checkpoints)]
    train_squares = jnp.stack([jnp.sum(item * item, axis=1) for item in train_proj])
    eval_squares = jnp.stack([jnp.sum(item * item, axis=1) for item in eval_proj])
    train_total, eval_total = lax.psum((train_squares, eval_squares), "ft")
    train_inv = lax.rsqrt(train_total / FEATURES + 1e-06)
    eval_inv = lax.rsqrt(eval_total / FEATURES + 1e-06)
    train_hats = [
        (train_proj[index] * train_inv[index][:, None]).astype(jnp.bfloat16)
        for index in range(checkpoints)
    ]
    eval_hats = [
        (eval_proj[index] * eval_inv[index][:, None]).astype(jnp.bfloat16)
        for index in range(checkpoints)
    ]
    eval_total_rows = eval_ids.shape[0] * lax.axis_size("ex")
    initial = jnp.zeros((train_ids.shape[0], eval_total_rows), jnp.float32)
    scores = initial
    for index in range(checkpoints):
        features_block = lax.all_gather(eval_hats[index], "ex", axis=0, tiled=True)
        fold_eval_block = lax.all_gather(eval_ids, "ex", axis=0, tiled=True)
        fold_scores_block = weights[index] * jnp.einsum(
            "ik,jk->ij", train_hats[index], features_block, preferred_element_type=jnp.float32
        )
        same_example = train_ids[:, None] == fold_eval_block[None, :]
        scores = add_block(scores, jnp.where(same_example, jnp.float32(0.0), fold_scores_block))
    return lax.psum_scatter(scores, "ft", scatter_dimension=1, tiled=True)


LINK = jnp.bfloat16
MESH_ID = pl.DeviceIdType.MESH
HIGHEST = lax.Precision.HIGHEST
OFFSETS = (2, 1, 3, 0)
CHUNKS = len(OFFSETS)
OWN = CHUNKS - 1
RAW = (0, 32, 64, 0)
PLAN = ((0, 0, 96), (1, 0, 80), (2, 0, 64), (3, 0, 48), (3, 96, 48))
STEPS = len(PLAN)
LANES = 128
TILE = 256


def coded(value):
    return (value * jnp.abs(value)).astype(LINK)


def decoded(code):
    wide = code.astype(jnp.float32)
    return wide * lax.rsqrt(jnp.maximum(jnp.abs(wide), jnp.float32(1e-36)))


def other(value):
    return 1 - value


def device_at(z, y, x, core):
    return ((z * 2 + y) * 2 + x) * 2 + core


def send(src, dst, send_sem, recv_sem, device):
    copy = pltpu.make_async_remote_copy(
        src_ref=src,
        dst_ref=dst,
        send_sem=send_sem,
        recv_sem=recv_sem,
        device_id={"ex": device},
        device_id_type=MESH_ID,
    )
    copy.start()
    return copy


def influence_kernel(
    train_ref,
    eval_ref,
    proj_ref,
    lr_ref,
    train_ids_ref,
    eval_ids_ref,
    out_ref,
    sketch,
    proj,
    s0,
    r0,
    keep,
    s1a,
    s1b,
    r1a,
    r1b,
    s2a,
    s2b,
    r2a,
    r2b,
    sz,
    rz,
    sraw,
    rraw,
    fin,
    scores_ref,
    p1,
    r1p,
    scaled_ref,
    p2,
    r2p,
    local_sem,
    pr_sem,
    s0_send,
    s0_recv,
    s1_send,
    s1_recv,
    s2_send,
    s2_recv,
    z_send,
    z_recv,
    raw_send,
    raw_recv,
    p1_send,
    p1_recv,
    p2_send,
    p2_recv,
    ready,
):
    me = lax.axis_index("ex")
    core = lax.rem(me, 2)
    x = lax.rem(me // 2, 2)
    y = lax.rem(me // 4, 2)
    z = me // 8
    sib = device_at(z, y, x, other(core))
    x_dev = device_at(z, y, other(x), core)
    y_dev = device_at(z, other(y), x, core)
    plane = [
        ((y + dy) % 2, (x + dx) % 2, (core + dc) % 2)
        for dy in range(2)
        for dx in range(2)
        for dc in range(2)
    ][:0:-1]
    checkpoints = lr_ref.shape[0]
    train_rows = train_ref.shape[1]
    eval_rows = eval_ref.shape[1]
    rows = train_rows + eval_rows
    block = keep.shape[3]
    half_cols = 4 * block
    zs = [lax.rem(z + offset, 4) for offset in OFFSETS]

    own_sketch = [
        pltpu.make_async_copy(train_ref, sketch.at[:, pl.ds(0, train_rows)], local_sem.at[0]),
        pltpu.make_async_copy(
            eval_ref, sketch.at[:, pl.ds(train_rows, eval_rows)], local_sem.at[1]
        ),
    ]
    for copy in own_sketch:
        copy.start()
    own_proj = []
    for at, side in enumerate((other(core), core)):
        for part in range(2):
            start = pl.multiple_of(side * half_cols + part * 2 * block, 2 * block)
            copy = pltpu.make_async_copy(
                proj_ref.at[:, pl.ds(start, 2 * block)], proj.at[at, part], pr_sem.at[at, part]
            )
            copy.start()
            own_proj.append(copy)

    below, above = z > 0, z < 3
    z_neighbours = below.astype(jnp.int32) + above.astype(jnp.int32)

    def signal(semaphore, device):
        pl.semaphore_signal(semaphore, inc=1, device_id={"ex": device}, device_id_type=MESH_ID)

    def signal_z(semaphore):
        @pl.when(below)
        def _():
            signal(semaphore, device_at(z - 1, y, x, core))

        @pl.when(above)
        def _():
            signal(semaphore, device_at(z + 1, y, x, core))

    barrier = pltpu.get_barrier_semaphore()
    for partner in (sib, x_dev, y_dev):
        signal(barrier, partner)
    signal_z(barrier)

    for copy in own_sketch:
        copy.wait()

    def products(k, at, store):
        per_part, per_block = 2 * block // TILE, block // TILE
        for tile in range(half_cols // TILE):
            part, first_col = tile // per_part, tile % per_part * TILE
            if k == 0 and first_col == 0:
                own_proj[2 * at + part].wait()
            total = jnp.dot(
                sketch[zs[k]],
                proj[at, part, :, first_col : first_col + TILE],
                preferred_element_type=jnp.float32,
            )
            store(k, tile // per_block, pl.ds(tile % per_block * TILE, TILE), total)

    def store_sent(k, to, cols, value):
        s0[k, to, :, cols] = coded(value)

    def store_kept(k, to, cols, value):
        keep[k, to, :, cols] = value

    s0_copies, s1_copies, s2_copies, z_copies, raw_copies = {}, {}, {}, {}, {}

    def swap(k):
        s0_copies[k] = send(s0.at[k], r0.at[k], s0_send.at[k], s0_recv.at[k], sib)

    def summed(k, at, part):
        return keep[k, at, part, :] + decoded(r0[k, at, part, :])

    def arrived(k):
        s0_copies[k].wait_recv()

    def forward(k):
        part = pl.ds(rows - RAW[k], RAW[k])
        place = pl.ds(0, RAW[k])
        for at in range(4):
            sraw[k - 1, at, place, :] = coded(summed(k, at, part))
        raw_copies[k] = send(
            sraw.at[k - 1, :, place],
            rraw.at[k - 1, :, place],
            raw_send.at[k - 1],
            raw_recv.at[k - 1],
            device_at(zs[k], y, x, core),
        )

    def parts(step):
        k, low, half = PLAN[step]
        return k, pl.ds(low, half), pl.ds(low + half, half), pl.ds(0, half)

    def first(step):
        k, part_a, part_b, place = parts(step)
        for slot, y_at in enumerate((other(y), y)):
            s1a[step, slot, place, :] = coded(summed(k, other(x) * 2 + y_at, part_a))
        copy_a = send(
            s1a.at[step, :, place],
            r1a.at[step, :, place],
            s1_send.at[0, step],
            s1_recv.at[0, step],
            x_dev,
        )
        for slot, x_at in enumerate((other(x), x)):
            s1b[step, slot, place, :] = coded(summed(k, x_at * 2 + other(y), part_b))
        copy_b = send(
            s1b.at[step, :, place],
            r1b.at[step, :, place],
            s1_send.at[1, step],
            s1_recv.at[1, step],
            y_dev,
        )
        for y_at in (other(y), y):
            keep[k, x * 2 + y_at, part_a, :] = summed(k, x * 2 + y_at, part_a)
        for x_at in (other(x), x):
            keep[k, x_at * 2 + y, part_b, :] = summed(k, x_at * 2 + y, part_b)
        s1_copies[step] = (copy_a, copy_b)

    def second(step):
        k, part_a, part_b, place = parts(step)
        s1_copies[step][0].wait_recv()
        s2a[step, place, :] = coded(
            keep[k, x * 2 + other(y), part_a, :] + decoded(r1a[step, 0, place, :])
        )
        copy_a = send(
            s2a.at[step, place], r2a.at[step, place], s2_send.at[0, step], s2_recv.at[0, step], y_dev
        )
        s1_copies[step][1].wait_recv()
        s2b[step, place, :] = coded(
            keep[k, other(x) * 2 + y, part_b, :] + decoded(r1b[step, 0, place, :])
        )
        copy_b = send(
            s2b.at[step, place], r2b.at[step, place], s2_send.at[1, step], s2_recv.at[1, step], x_dev
        )
        keep[k, x * 2 + y, part_a, :] += decoded(r1a[step, 1, place, :])
        keep[k, x * 2 + y, part_b, :] += decoded(r1b[step, 1, place, :])
        s2_copies[step] = (copy_a, copy_b)

    def third(step):
        k, part_a, part_b, place = parts(step)
        for copy, received, part in zip(s2_copies[step], (r2a, r2b), (part_a, part_b)):
            copy.wait_recv()
            value = keep[k, x * 2 + y, part, :] + decoded(received[step, place, :])
            if k == OWN:
                fin[part, :] = value
            else:
                sz[k, part, :] = coded(value)
        if k != OWN:
            sent = pl.ds(0, rows - RAW[k])
            z_copies[k] = send(
                sz.at[k, sent],
                rz.at[k, sent],
                z_send.at[k],
                z_recv.at[k],
                device_at(zs[k], y, x, core),
            )

    def add_raw():
        for k in raw_copies:
            raw_copies[k].wait_recv()
            part = pl.ds(rows - RAW[k], RAW[k])
            for at in range(4):
                keep[OWN, at, part, :] += decoded(rraw[k - 1, at, pl.ds(0, RAW[k]), :])

    products(0, 0, store_sent)
    products(0, 1, store_kept)
    pl.semaphore_wait(barrier, 3 + z_neighbours)
    signal_z(ready.at[0])
    swap(0)
    products(1, 0, store_sent)
    swap(1)
    arrived(0)
    first(0)
    pl.semaphore_wait(ready.at[0], z_neighbours)
    signal_z(ready.at[1])
    products(1, 1, store_kept)
    products(2, 0, store_sent)
    swap(2)
    arrived(1)
    first(1)
    products(2, 1, store_kept)
    pl.semaphore_wait(ready.at[1], z_neighbours)
    forward(1)
    arrived(2)
    forward(2)
    products(3, 0, store_sent)
    swap(3)
    second(0)
    first(2)
    products(3, 1, store_kept)
    arrived(3)
    second(1)
    third(0)
    add_raw()
    second(2)
    first(3)
    first(4)
    third(1)
    second(3)
    third(2)
    second(4)
    third(3)
    for k in z_copies:
        z_copies[k].wait_recv()
    third(4)
    for k in z_copies:
        part = pl.ds(0, rows - RAW[k])
        fin[part, :] += decoded(rz[k, part, :])

    train = fin[pl.ds(0, train_rows), :]
    evals = fin[pl.ds(train_rows, eval_rows), :]
    contract = (((1,), (1,)), ((), ()))

    def dot(left, right):
        return lax.dot_general(
            left, right, contract, precision=HIGHEST, preferred_element_type=jnp.float32
        )

    scores_ref[...] = dot(train, evals)
    ones = jnp.ones((8, block), jnp.float32)
    train_squares = dot(ones, train * train)
    eval_squares = dot(ones, evals * evals)
    row8 = lax.broadcasted_iota(jnp.int32, (8, LANES), 0)
    lane8 = lax.broadcasted_iota(jnp.int32, (8, LANES), 1)
    shared = jnp.where(row8 == 3, eval_squares, jnp.float32(0.0))
    own_ids = eval_ids_ref.shape[0]
    for at in range(own_ids):
        place = (row8 == 2) & (lane8 == me * own_ids + at)
        shared = jnp.where(place, eval_ids_ref[at].astype(jnp.float32), shared)
    for p in range(8):
        for z_at in range(4):
            low = z_at * 16 + p * 2
            p1[p, 0, z_at * 2 : z_at * 2 + 2, :] = scores_ref[low : low + 2, :]
        p1[p, 1] = shared
        p1[p, 1, 4:5, 0:train_rows] = train_squares[0:1, :]

    p1_copies = []
    for at, (y_at, x_at, core_at) in enumerate(plane):
        p1_copies.append(
            send(
                p1.at[(y_at * 2 + x_at) * 2 + core_at],
                r1p.at[at],
                p1_send.at[at],
                p1_recv.at[at],
                device_at(z, y_at, x_at, core_at),
            )
        )
    total = p1[lax.rem(me, 8)]
    for at, copy in reversed(list(enumerate(p1_copies))):
        copy.wait_recv()
        total = total + r1p[at]
    shared = total[1]
    owner_lane = row8 // 2 * 16 + lax.rem(me, 8) * 2 + row8 % 2
    train_square = jnp.sum(
        jnp.where(lane8 == owner_lane, shared[4:5, :], jnp.float32(0.0)), axis=1, keepdims=True
    )
    weight = lr_ref[z].astype(jnp.float32) / FEATURES
    train_inv = lax.rsqrt(train_square / FEATURES + 1e-06)
    eval_inv = lax.rsqrt(shared[3:4, :] / FEATURES + 1e-06)
    scaled_ref[...] = weight * (total[0] * train_inv * eval_inv)
    for z_at in range(4):
        p2[z_at] = shared
        p2[z_at, 0:2, :] = scaled_ref[2 * z_at : 2 * z_at + 2, :]
    p2_copies = []
    for at in range(3):
        to = lax.rem(z + at + 1, 4)
        p2_copies.append(
            send(
                p2.at[to], r2p.at[at], p2_send.at[at], p2_recv.at[at], device_at(to, y, x, core)
            )
        )
    total = p2[z]
    for at, copy in enumerate(p2_copies):
        copy.wait_recv()
        total = total + r2p[at]
    row2 = lax.broadcasted_iota(jnp.int32, (2, LANES), 0)
    own = jnp.where(
        row2 == 0, train_ids_ref[0].astype(jnp.float32), train_ids_ref[1].astype(jnp.float32)
    )
    out_ref[...] = jnp.where(own == total[2:3, :], jnp.float32(0.0), total[0:2, :])

    for copy in p1_copies + p2_copies:
        copy.wait_send()
    for step in range(STEPS):
        for copy in s1_copies[step] + s2_copies[step]:
            copy.wait_send()
    for group in (s0_copies, z_copies, raw_copies):
        for k in group:
            group[k].wait_send()


def fused(train_sketch, eval_sketch, projection, lr_weight, train_ids, eval_ids):
    checkpoints, train_rows, depth = train_sketch.shape
    eval_rows = eval_sketch.shape[1]
    rows = train_rows + eval_rows
    half = rows // 2
    block = projection.shape[1] // 8
    anywhere = pl.BlockSpec(memory_space=pl.ANY)
    scalars = pl.BlockSpec(memory_space=pltpu.SMEM)
    dma = pltpu.SemaphoreType.DMA
    f32, bf16 = jnp.float32, jnp.bfloat16
    return pl.pallas_call(
        influence_kernel,
        out_shape=jax.ShapeDtypeStruct((train_ids.shape[0], eval_rows), f32),
        in_specs=[anywhere] * 3 + [scalars] * 3,
        out_specs=pl.BlockSpec(memory_space=pltpu.VMEM),
        scratch_shapes=[
            pltpu.VMEM((checkpoints, rows, depth), bf16),
            pltpu.VMEM((2, 2, depth, 2 * block), bf16),
            pltpu.VMEM((checkpoints, 4, rows, block), LINK),
            pltpu.VMEM((checkpoints, 4, rows, block), LINK),
            pltpu.VMEM((checkpoints, 4, rows, block), f32),
            pltpu.VMEM((STEPS, 2, half, block), LINK),
            pltpu.VMEM((STEPS, 2, half, block), LINK),
            pltpu.VMEM((STEPS, 2, half, block), LINK),
            pltpu.VMEM((STEPS, 2, half, block), LINK),
            pltpu.VMEM((STEPS, half, block), LINK),
            pltpu.VMEM((STEPS, half, block), LINK),
            pltpu.VMEM((STEPS, half, block), LINK),
            pltpu.VMEM((STEPS, half, block), LINK),
            pltpu.VMEM((3, rows, block), LINK),
            pltpu.VMEM((3, rows, block), LINK),
            pltpu.VMEM((2, 4, max(RAW), block), LINK),
            pltpu.VMEM((2, 4, max(RAW), block), LINK),
            pltpu.VMEM((rows, block), f32),
            pltpu.VMEM((train_rows, LANES), f32),
            pltpu.VMEM((8, 2, 8, LANES), f32),
            pltpu.VMEM((7, 2, 8, LANES), f32),
            pltpu.VMEM((8, LANES), f32),
            pltpu.VMEM((4, 8, LANES), f32),
            pltpu.VMEM((3, 8, LANES), f32),
            dma((2,)),
            dma((2, 2)),
            dma((CHUNKS,)),
            dma((CHUNKS,)),
            dma((2, STEPS)),
            dma((2, STEPS)),
            dma((2, STEPS)),
            dma((2, STEPS)),
            dma((3,)),
            dma((3,)),
            dma((2,)),
            dma((2,)),
            dma((7,)),
            dma((7,)),
            dma((3,)),
            dma((3,)),
            pltpu.SemaphoreType.REGULAR((2,)),
        ],
        compiler_params=pltpu.CompilerParams(
            collective_id=0, has_side_effects=True, vmem_limit_bytes=60 * 1024 * 1024
        ),
    )(
        train_sketch,
        eval_sketch,
        projection,
        lr_weight,
        train_ids,
        eval_ids,
    )


def planned(mesh):
    def body(train_sketch, eval_sketch, projection, lr_weight, train_ids, eval_ids):
        arrays = (train_sketch, eval_sketch, projection, lr_weight, train_ids, eval_ids)
        sizes = (mesh.shape["grp"], mesh.shape["ex"], mesh.shape["ft"])
        fits = (
            sizes == (1, 32, 1)
            and train_sketch.shape[:2] == (4, 64)
            and eval_sketch.shape[:2] == (4, 128)
            and projection.shape[1] == FEATURES
        )
        return fused(*arrays) if fits else shards(*arrays)

    return body


def solution(mesh):
    body = planned(mesh)
    return jax.shard_map(
        body,
        mesh=mesh,
        in_specs=(
            P(None, "grp", "ex"),
            P(None, "grp", "ex"),
            P("ex", "ft"),
            P(),
            P(("grp", "ex")),
            P(("grp", "ex")),
        ),
        out_specs=P(("grp", "ex"), "ft"),
        check_vma=False,
    )
```

```python
import functools

import jax
import jax.numpy as jnp
from jax import lax
from jax.experimental import pallas as pl
from jax.experimental.pallas import tpu as pltpu
from jax.sharding import PartitionSpec as P

FEATURES = 4096


def project(sketch, projection):
    return lax.psum_scatter(
        jnp.dot(sketch, projection, preferred_element_type=jnp.float32),
        "ex",
        scatter_dimension=0,
        tiled=True,
    )


def add_block(totals, scores_block):
    return totals + scores_block


def shards(train_sketch, eval_sketch, projection, lr_weight, train_ids, eval_ids):
    checkpoints = train_sketch.shape[0]
    weights = lr_weight.astype(jnp.float32) / FEATURES
    train_proj = [project(train_sketch[index], projection) for index in range(checkpoints)]
    eval_proj = [project(eval_sketch[index], projection) for index in range(checkpoints)]
    train_squares = jnp.stack([jnp.sum(item * item, axis=1) for item in train_proj])
    eval_squares = jnp.stack([jnp.sum(item * item, axis=1) for item in eval_proj])
    train_total, eval_total = lax.psum((train_squares, eval_squares), "ft")
    train_inv = lax.rsqrt(train_total / FEATURES + 1e-06)
    eval_inv = lax.rsqrt(eval_total / FEATURES + 1e-06)
    train_hats = [
        (train_proj[index] * train_inv[index][:, None]).astype(jnp.bfloat16)
        for index in range(checkpoints)
    ]
    eval_hats = [
        (eval_proj[index] * eval_inv[index][:, None]).astype(jnp.bfloat16)
        for index in range(checkpoints)
    ]
    eval_total_rows = eval_ids.shape[0] * lax.axis_size("ex")
    initial = jnp.zeros((train_ids.shape[0], eval_total_rows), jnp.float32)
    scores = initial
    for index in range(checkpoints):
        features_block = lax.all_gather(eval_hats[index], "ex", axis=0, tiled=True)
        fold_eval_block = lax.all_gather(eval_ids, "ex", axis=0, tiled=True)
        fold_scores_block = weights[index] * jnp.einsum(
            "ik,jk->ij", train_hats[index], features_block, preferred_element_type=jnp.float32
        )
        same_example = train_ids[:, None] == fold_eval_block[None, :]
        scores = add_block(scores, jnp.where(same_example, jnp.float32(0.0), fold_scores_block))
    return lax.psum_scatter(scores, "ft", scatter_dimension=1, tiled=True)


LINK = jnp.bfloat16
MESH_ID = pl.DeviceIdType.MESH
HIGHEST = lax.Precision.HIGHEST
OFFSETS = (2, 1, 3, 0)
CHUNKS = len(OFFSETS)
OWN = CHUNKS - 1
RAW = (0, 32, 64, 0)
PLAN = ((0, 0, 96), (1, 0, 80), (2, 0, 64), (3, 0, 48), (3, 96, 48))
STEPS = len(PLAN)
LANES = 128
TILE = 256


def coded(value):
    return (value * jnp.abs(value)).astype(LINK)


def decoded(code):
    wide = code.astype(jnp.float32)
    return wide * lax.rsqrt(jnp.maximum(jnp.abs(wide), jnp.float32(1e-36)))


def other(value):
    return 1 - value


def device_at(z, y, x, core):
    return ((z * 2 + y) * 2 + x) * 2 + core


def send(src, dst, send_sem, recv_sem, device):
    copy = pltpu.make_async_remote_copy(
        src_ref=src,
        dst_ref=dst,
        send_sem=send_sem,
        recv_sem=recv_sem,
        device_id={"ex": device},
        device_id_type=MESH_ID,
    )
    copy.start()
    return copy


def influence_kernel(
    train_ref,
    eval_ref,
    proj_ref,
    lr_ref,
    train_ids_ref,
    eval_ids_ref,
    out_ref,
    sketch,
    proj,
    s0,
    r0,
    keep,
    s1a,
    s1b,
    r1a,
    r1b,
    s2a,
    s2b,
    r2a,
    r2b,
    sz,
    rz,
    sraw,
    rraw,
    fin,
    scores_ref,
    p1,
    r1p,
    scaled_ref,
    p2,
    r2p,
    local_sem,
    pr_sem,
    s0_send,
    s0_recv,
    s1_send,
    s1_recv,
    s2_send,
    s2_recv,
    z_send,
    z_recv,
    raw_send,
    raw_recv,
    p1_send,
    p1_recv,
    p2_send,
    p2_recv,
    ready,
):
    me = lax.axis_index("ex")
    core = lax.rem(me, 2)
    x = lax.rem(me // 2, 2)
    y = lax.rem(me // 4, 2)
    z = me // 8
    sib = device_at(z, y, x, other(core))
    x_dev = device_at(z, y, other(x), core)
    y_dev = device_at(z, other(y), x, core)
    plane = [
        ((y + dy) % 2, (x + dx) % 2, (core + dc) % 2)
        for dy in range(2)
        for dx in range(2)
        for dc in range(2)
    ][:0:-1]
    checkpoints = lr_ref.shape[0]
    train_rows = train_ref.shape[1]
    eval_rows = eval_ref.shape[1]
    rows = train_rows + eval_rows
    block = keep.shape[3]
    half_cols = 4 * block
    zs = [lax.rem(z + offset, 4) for offset in OFFSETS]

    own_sketch = [
        pltpu.make_async_copy(train_ref, sketch.at[:, pl.ds(0, train_rows)], local_sem.at[0]),
        pltpu.make_async_copy(
            eval_ref, sketch.at[:, pl.ds(train_rows, eval_rows)], local_sem.at[1]
        ),
    ]
    for copy in own_sketch:
        copy.start()
    own_proj = []
    for at, side in enumerate((other(core), core)):
        for part in range(2):
            start = pl.multiple_of(side * half_cols + part * 2 * block, 2 * block)
            copy = pltpu.make_async_copy(
                proj_ref.at[:, pl.ds(start, 2 * block)], proj.at[at, part], pr_sem.at[at, part]
            )
            copy.start()
            own_proj.append(copy)

    below, above = z > 0, z < 3
    z_neighbours = below.astype(jnp.int32) + above.astype(jnp.int32)

    def signal(semaphore, device):
        pl.semaphore_signal(semaphore, inc=1, device_id={"ex": device}, device_id_type=MESH_ID)

    def signal_z(semaphore):
        @pl.when(below)
        def _():
            signal(semaphore, device_at(z - 1, y, x, core))

        @pl.when(above)
        def _():
            signal(semaphore, device_at(z + 1, y, x, core))

    barrier = pltpu.get_barrier_semaphore()
    for partner in (sib, x_dev, y_dev):
        signal(barrier, partner)
    signal_z(barrier)

    for copy in own_sketch:
        copy.wait()

    def products(k, at, store):
        per_part, per_block = 2 * block // TILE, block // TILE
        for tile in range(half_cols // TILE):
            part, first_col = tile // per_part, tile % per_part * TILE
            if k == 0 and first_col == 0:
                own_proj[2 * at + part].wait()
            total = jnp.dot(
                sketch[zs[k]],
                proj[at, part, :, first_col : first_col + TILE],
                preferred_element_type=jnp.float32,
            )
            store(k, tile // per_block, pl.ds(tile % per_block * TILE, TILE), total)

    def store_sent(k, to, cols, value):
        s0[k, to, :, cols] = coded(value)

    def store_kept(k, to, cols, value):
        keep[k, to, :, cols] = value

    s0_copies, s1_copies, s2_copies, z_copies, raw_copies = {}, {}, {}, {}, {}

    def swap(k):
        s0_copies[k] = send(s0.at[k], r0.at[k], s0_send.at[k], s0_recv.at[k], sib)

    def summed(k, at, part):
        return keep[k, at, part, :] + decoded(r0[k, at, part, :])

    def arrived(k):
        s0_copies[k].wait_recv()

    def forward(k):
        part = pl.ds(rows - RAW[k], RAW[k])
        place = pl.ds(0, RAW[k])
        for at in range(4):
            sraw[k - 1, at, place, :] = coded(summed(k, at, part))
        raw_copies[k] = send(
            sraw.at[k - 1, :, place],
            rraw.at[k - 1, :, place],
            raw_send.at[k - 1],
            raw_recv.at[k - 1],
            device_at(zs[k], y, x, core),
        )

    def parts(step):
        k, low, half = PLAN[step]
        return k, pl.ds(low, half), pl.ds(low + half, half), pl.ds(0, half)

    def first(step):
        k, part_a, part_b, place = parts(step)
        for slot, y_at in enumerate((other(y), y)):
            s1a[step, slot, place, :] = coded(summed(k, other(x) * 2 + y_at, part_a))
        copy_a = send(
            s1a.at[step, :, place],
            r1a.at[step, :, place],
            s1_send.at[0, step],
            s1_recv.at[0, step],
            x_dev,
        )
        for slot, x_at in enumerate((other(x), x)):
            s1b[step, slot, place, :] = coded(summed(k, x_at * 2 + other(y), part_b))
        copy_b = send(
            s1b.at[step, :, place],
            r1b.at[step, :, place],
            s1_send.at[1, step],
            s1_recv.at[1, step],
            y_dev,
        )
        for y_at in (other(y), y):
            keep[k, x * 2 + y_at, part_a, :] = summed(k, x * 2 + y_at, part_a)
        for x_at in (other(x), x):
            keep[k, x_at * 2 + y, part_b, :] = summed(k, x_at * 2 + y, part_b)
        s1_copies[step] = (copy_a, copy_b)

    def second(step):
        k, part_a, part_b, place = parts(step)
        s1_copies[step][0].wait_recv()
        s2a[step, place, :] = coded(
            keep[k, x * 2 + other(y), part_a, :] + decoded(r1a[step, 0, place, :])
        )
        copy_a = send(
            s2a.at[step, place], r2a.at[step, place], s2_send.at[0, step], s2_recv.at[0, step], y_dev
        )
        s1_copies[step][1].wait_recv()
        s2b[step, place, :] = coded(
            keep[k, other(x) * 2 + y, part_b, :] + decoded(r1b[step, 0, place, :])
        )
        copy_b = send(
            s2b.at[step, place], r2b.at[step, place], s2_send.at[1, step], s2_recv.at[1, step], x_dev
        )
        keep[k, x * 2 + y, part_a, :] += decoded(r1a[step, 1, place, :])
        keep[k, x * 2 + y, part_b, :] += decoded(r1b[step, 1, place, :])
        s2_copies[step] = (copy_a, copy_b)

    def third(step):
        k, part_a, part_b, place = parts(step)
        for copy, received, part in zip(s2_copies[step], (r2a, r2b), (part_a, part_b)):
            copy.wait_recv()
            value = keep[k, x * 2 + y, part, :] + decoded(received[step, place, :])
            if k == OWN:
                fin[part, :] = value
            else:
                sz[k, part, :] = coded(value)
        if k != OWN:
            sent = pl.ds(0, rows - RAW[k])
            z_copies[k] = send(
                sz.at[k, sent],
                rz.at[k, sent],
                z_send.at[k],
                z_recv.at[k],
                device_at(zs[k], y, x, core),
            )

    def add_raw():
        for k in raw_copies:
            raw_copies[k].wait_recv()
            part = pl.ds(rows - RAW[k], RAW[k])
            for at in range(4):
                keep[OWN, at, part, :] += decoded(rraw[k - 1, at, pl.ds(0, RAW[k]), :])

    products(0, 0, store_sent)
    pl.semaphore_wait(barrier, 3 + z_neighbours)
    signal_z(ready.at[0])
    swap(0)
    products(0, 1, store_kept)
    products(1, 0, store_sent)
    swap(1)
    arrived(0)
    first(0)
    products(1, 1, store_kept)
    products(2, 0, store_sent)
    swap(2)
    arrived(1)
    first(1)
    pl.semaphore_wait(ready.at[0], z_neighbours)
    signal_z(ready.at[1])
    products(2, 1, store_kept)
    products(3, 0, store_sent)
    arrived(2)
    swap(3)
    pl.semaphore_wait(ready.at[1], z_neighbours)
    forward(2)
    forward(1)
    second(0)
    first(2)
    products(3, 1, store_kept)
    arrived(3)
    second(1)
    third(0)
    add_raw()
    second(2)
    first(3)
    first(4)
    third(1)
    second(3)
    third(2)
    second(4)
    third(3)
    third(4)
    for k in z_copies:
        z_copies[k].wait_recv()
        part = pl.ds(0, rows - RAW[k])
        fin[part, :] += decoded(rz[k, part, :])

    train = fin[pl.ds(0, train_rows), :]
    evals = fin[pl.ds(train_rows, eval_rows), :]
    contract = (((1,), (1,)), ((), ()))

    def dot(left, right):
        return lax.dot_general(
            left, right, contract, precision=HIGHEST, preferred_element_type=jnp.float32
        )

    scores_ref[...] = dot(train, evals)
    ones = jnp.ones((8, block), jnp.float32)
    train_squares = dot(ones, train * train)
    eval_squares = dot(ones, evals * evals)
    row8 = lax.broadcasted_iota(jnp.int32, (8, LANES), 0)
    lane8 = lax.broadcasted_iota(jnp.int32, (8, LANES), 1)
    shared = jnp.where(row8 == 3, eval_squares, jnp.float32(0.0))
    own_ids = eval_ids_ref.shape[0]
    for at in range(own_ids):
        place = (row8 == 2) & (lane8 == me * own_ids + at)
        shared = jnp.where(place, eval_ids_ref[at].astype(jnp.float32), shared)
    for p in range(8):
        for z_at in range(4):
            low = z_at * 16 + p * 2
            p1[p, 0, z_at * 2 : z_at * 2 + 2, :] = scores_ref[low : low + 2, :]
        p1[p, 1] = shared
        p1[p, 1, 4:5, 0:train_rows] = train_squares[0:1, :]

    p1_copies = []
    for at, (y_at, x_at, core_at) in enumerate(plane):
        p1_copies.append(
            send(
                p1.at[(y_at * 2 + x_at) * 2 + core_at],
                r1p.at[at],
                p1_send.at[at],
                p1_recv.at[at],
                device_at(z, y_at, x_at, core_at),
            )
        )
    total = p1[lax.rem(me, 8)]
    for at, copy in reversed(list(enumerate(p1_copies))):
        copy.wait_recv()
        total = total + r1p[at]
    shared = total[1]
    owner_lane = row8 // 2 * 16 + lax.rem(me, 8) * 2 + row8 % 2
    train_square = jnp.sum(
        jnp.where(lane8 == owner_lane, shared[4:5, :], jnp.float32(0.0)), axis=1, keepdims=True
    )
    weight = lr_ref[z].astype(jnp.float32) / FEATURES
    train_inv = lax.rsqrt(train_square / FEATURES + 1e-06)
    eval_inv = lax.rsqrt(shared[3:4, :] / FEATURES + 1e-06)
    scaled_ref[...] = weight * (total[0] * train_inv * eval_inv)
    for z_at in range(4):
        p2[z_at] = shared
        p2[z_at, 0:2, :] = scaled_ref[2 * z_at : 2 * z_at + 2, :]
    p2_copies = []
    for at in range(3):
        to = lax.rem(z + at + 1, 4)
        p2_copies.append(
            send(
                p2.at[to], r2p.at[at], p2_send.at[at], p2_recv.at[at], device_at(to, y, x, core)
            )
        )
    total = p2[z]
    for at, copy in enumerate(p2_copies):
        copy.wait_recv()
        total = total + r2p[at]
    row2 = lax.broadcasted_iota(jnp.int32, (2, LANES), 0)
    own = jnp.where(
        row2 == 0, train_ids_ref[0].astype(jnp.float32), train_ids_ref[1].astype(jnp.float32)
    )
    out_ref[...] = jnp.where(own == total[2:3, :], jnp.float32(0.0), total[0:2, :])

    for copy in p1_copies + p2_copies:
        copy.wait_send()
    for step in range(STEPS):
        for copy in s1_copies[step] + s2_copies[step]:
            copy.wait_send()
    for group in (s0_copies, z_copies, raw_copies):
        for k in group:
            group[k].wait_send()


def fused(train_sketch, eval_sketch, projection, lr_weight, train_ids, eval_ids):
    checkpoints, train_rows, depth = train_sketch.shape
    eval_rows = eval_sketch.shape[1]
    rows = train_rows + eval_rows
    half = rows // 2
    block = projection.shape[1] // 8
    anywhere = pl.BlockSpec(memory_space=pl.ANY)
    scalars = pl.BlockSpec(memory_space=pltpu.SMEM)
    dma = pltpu.SemaphoreType.DMA
    f32, bf16 = jnp.float32, jnp.bfloat16
    return pl.pallas_call(
        influence_kernel,
        out_shape=jax.ShapeDtypeStruct((train_ids.shape[0], eval_rows), f32),
        in_specs=[anywhere] * 3 + [scalars] * 3,
        out_specs=pl.BlockSpec(memory_space=pltpu.VMEM),
        scratch_shapes=[
            pltpu.VMEM((checkpoints, rows, depth), bf16),
            pltpu.VMEM((2, 2, depth, 2 * block), bf16),
            pltpu.VMEM((checkpoints, 4, rows, block), LINK),
            pltpu.VMEM((checkpoints, 4, rows, block), LINK),
            pltpu.VMEM((checkpoints, 4, rows, block), f32),
            pltpu.VMEM((STEPS, 2, half, block), LINK),
            pltpu.VMEM((STEPS, 2, half, block), LINK),
            pltpu.VMEM((STEPS, 2, half, block), LINK),
            pltpu.VMEM((STEPS, 2, half, block), LINK),
            pltpu.VMEM((STEPS, half, block), LINK),
            pltpu.VMEM((STEPS, half, block), LINK),
            pltpu.VMEM((STEPS, half, block), LINK),
            pltpu.VMEM((STEPS, half, block), LINK),
            pltpu.VMEM((3, rows, block), LINK),
            pltpu.VMEM((3, rows, block), LINK),
            pltpu.VMEM((2, 4, max(RAW), block), LINK),
            pltpu.VMEM((2, 4, max(RAW), block), LINK),
            pltpu.VMEM((rows, block), f32),
            pltpu.VMEM((train_rows, LANES), f32),
            pltpu.VMEM((8, 2, 8, LANES), f32),
            pltpu.VMEM((7, 2, 8, LANES), f32),
            pltpu.VMEM((8, LANES), f32),
            pltpu.VMEM((4, 8, LANES), f32),
            pltpu.VMEM((3, 8, LANES), f32),
            dma((2,)),
            dma((2, 2)),
            dma((CHUNKS,)),
            dma((CHUNKS,)),
            dma((2, STEPS)),
            dma((2, STEPS)),
            dma((2, STEPS)),
            dma((2, STEPS)),
            dma((3,)),
            dma((3,)),
            dma((2,)),
            dma((2,)),
            dma((7,)),
            dma((7,)),
            dma((3,)),
            dma((3,)),
            pltpu.SemaphoreType.REGULAR((2,)),
        ],
        compiler_params=pltpu.CompilerParams(
            collective_id=0, has_side_effects=True, vmem_limit_bytes=60 * 1024 * 1024
        ),
    )(
        train_sketch,
        eval_sketch,
        projection,
        lr_weight,
        train_ids,
        eval_ids,
    )


def planned(mesh):
    def body(train_sketch, eval_sketch, projection, lr_weight, train_ids, eval_ids):
        arrays = (train_sketch, eval_sketch, projection, lr_weight, train_ids, eval_ids)
        sizes = (mesh.shape["grp"], mesh.shape["ex"], mesh.shape["ft"])
        fits = (
            sizes == (1, 32, 1)
            and train_sketch.shape[:2] == (4, 64)
            and eval_sketch.shape[:2] == (4, 128)
            and projection.shape[1] == FEATURES
        )
        return fused(*arrays) if fits else shards(*arrays)

    return body


def solution(mesh):
    body = planned(mesh)
    return jax.shard_map(
        body,
        mesh=mesh,
        in_specs=(
            P(None, "grp", "ex"),
            P(None, "grp", "ex"),
            P("ex", "ft"),
            P(),
            P(("grp", "ex")),
            P(("grp", "ex")),
        ),
        out_specs=P(("grp", "ex"), "ft"),
        check_vma=False,
    )
```
